32 devices in a mesh: parts: 2 (over y), hold: 16 (over z, x, core).
Axes of the slice: x: 2, y: 2, z: 4, core: 2. Of those that a mesh axis runs over, the one named last changes fastest.
Arguments:
- embeddings: float32 [16384, 768], P(('parts', 'hold')), parts along dimension 0
- cluster_id: int32 [16384], P(('parts', 'hold')), parts along dimension 0, may hold values from 0 to 127, as said below
- cluster_rank: int32 [16384], P(('parts', 'hold')), parts along dimension 0, may hold values from 0 to 767, as said below
Outputs:
- maxima: float32 [16384], P(('parts', 'hold')), parts along dimension 0
The draws below stay inside these ranges and needn't reach their ends.
There are 2 independent parts, one for each index of `parts`. The reference program is written for one: setup_inputs(seed, part) draws one part's arguments, and reference() takes and returns one part's arrays. A program takes and returns all parts, laid end to end along the dimension named above; each array names one. Nothing has to cross between parts.
Inputs may be any that keep to these rules, and one draw needn't show every extreme that they name: `cluster_id`: clusters 8 * j to 8 * j + 7 form owner block j. The rows of one device fall into any one owner block at most 48 times; in every draw one owner block gets exactly 48 rows from every device. `cluster_rank`: within each cluster the ranks of its rows are 0 to its size - 1, each once. No cluster has more than 16 * 48 rows; in every draw one cluster has exactly that many.
All inputs are finite; a program needn't handle non-finite values.
Results may differ from the reference program's by a relative error of at most 0.0003.
Values may be sent and summed in bfloat16 or wider, within the bound.
A program may use at most 64 MiB of HBM per device.

```python
import math
import jax
import jax.numpy as jnp
from jax import lax

D = 768
ROWS_DEV = 512
CL_DEV = 8
SLOT = 48
CLUSTERS = 128
TOTAL = 8192
N_HOLD = 16


def layout(key):
    holders = N_HOLD
    own_rows = ROWS_DEV
    slot_count = SLOT
    busiest = jax.random.randint(jax.random.fold_in(key, 11), (), 0, holders)
    columns = jnp.arange(holders, dtype=jnp.int32)
    random_ints = jax.random.randint(jax.random.fold_in(key, 12), (holders, holders), 0, 1 << 20)
    priority = jnp.where(columns[None, :] == busiest, -1, random_ints * holders + columns[None, :])
    ranking = jnp.argsort(priority, axis=1).astype(jnp.int32)
    row_index = jnp.arange(own_rows, dtype=jnp.int32)
    filled = holders // 4
    part_rows = filled * slot_count
    position = jnp.where(row_index < part_rows, row_index // slot_count, filled + (row_index - part_rows) % (holders - filled))
    shuffle_ints = jax.random.randint(jax.random.fold_in(key, 13), (holders, own_rows), 0, 1 << 16)
    shuffle = jnp.argsort(shuffle_ints * own_rows + row_index[None, :], axis=1).astype(jnp.int32)
    position = position[shuffle]
    owners = jnp.take_along_axis(ranking, position, axis=1)
    first_pick = jax.random.randint(jax.random.fold_in(key, 14), (holders, own_rows), 0, CL_DEV)
    second = jax.random.randint(jax.random.fold_in(key, 15), (holders, own_rows), 0, CL_DEV)
    offset = jax.random.randint(jax.random.fold_in(key, 16), (holders,), 0, CL_DEV)
    local_pick = (jnp.minimum(first_pick, second) + offset[owners]) % CL_DEV
    local_pick = jnp.where(owners == busiest, offset[busiest], local_pick)
    cluster = (owners * CL_DEV + local_pick).reshape(-1).astype(jnp.int32)
    total_rows = holders * own_rows
    tie_break = jax.random.permutation(jax.random.fold_in(key, 17), total_rows).astype(jnp.int32)
    sort_key = cluster * total_rows + tie_break
    sorting = jnp.argsort(sort_key).astype(jnp.int32)
    sorted_labels = cluster[sorting]
    spots = jnp.arange(total_rows, dtype=jnp.int32)
    changes = jnp.concatenate([jnp.ones((1,), bool), sorted_labels[1:] != sorted_labels[:-1]])
    openings = jnp.where(changes, spots, 0)
    cluster_start = lax.cummax(openings)
    rank_values = jnp.zeros((total_rows,), jnp.int32).at[sorting].set(spots - cluster_start)
    return (cluster, rank_values)


def draw_cluster_id(key, part):
    cluster, rank_values = layout(key)
    return cluster


def draw_cluster_rank(key, part):
    cluster, rank_values = layout(key)
    return rank_values


def draw_embeddings(key, part):
    cluster, rank_values = layout(key)
    key = jax.random.fold_in(key, 3)
    centres = jax.random.normal(jax.random.fold_in(key, 1), (CLUSTERS, D), jnp.float32)
    spread = jnp.exp(jax.random.uniform(jax.random.fold_in(key, 2), (TOTAL, 1), jnp.float32, math.log(0.25), math.log(3.0)))
    jitter = jax.random.normal(jax.random.fold_in(key, 4), (TOTAL, D), jnp.float32)
    return centres[cluster] + spread * jitter


def setup_inputs(seed: int = 0, part: int = 0) -> dict:
    splits = jax.random.split(jax.random.key(seed), 4)
    own_keys = jax.random.split(jax.random.fold_in(splits[3], part), 4)
    embeddings = draw_embeddings(jax.random.fold_in(jax.random.fold_in(splits[3], part), 71), part)
    cluster_id = draw_cluster_id(jax.random.fold_in(jax.random.fold_in(splits[3], part), 71), part)
    cluster_rank = draw_cluster_rank(jax.random.fold_in(jax.random.fold_in(splits[3], part), 71), part)
    return dict(embeddings=embeddings, cluster_id=cluster_id, cluster_rank=cluster_rank)


def reference(embeddings, cluster_id, cluster_rank):
    total_rows = embeddings.shape[0]
    squares = lax.optimization_barrier(jnp.sum(embeddings * embeddings, axis=1, keepdims=True))
    normed = (embeddings * lax.rsqrt(squares + 1e-06)).astype(jnp.bfloat16)
    sort_key = cluster_id.astype(jnp.int32) * total_rows + cluster_rank.astype(jnp.int32)
    sorting = jnp.argsort(sort_key).astype(jnp.int32)
    sorted_rows = normed[sorting]
    sorted_labels = cluster_id[sorting].astype(jnp.int32)
    sorted_orders = cluster_rank[sorting].astype(jnp.int32)
    reach = N_HOLD * SLOT
    block_rows = 512
    padded_rows = jnp.concatenate([jnp.zeros((reach, sorted_rows.shape[1]), sorted_rows.dtype), sorted_rows], axis=0)
    padded_labels = jnp.concatenate([jnp.full((reach,), -1, jnp.int32), sorted_labels], axis=0)
    padded_orders = jnp.concatenate([jnp.full((reach,), -1, jnp.int32), sorted_orders], axis=0)

    def one_block(offset):
        queries = lax.dynamic_slice_in_dim(sorted_rows, offset, block_rows, 0).astype(jnp.float32)
        keys = lax.dynamic_slice_in_dim(padded_rows, offset, reach + block_rows, 0).astype(jnp.float32)
        scores = jnp.dot(queries, keys.T, preferred_element_type=jnp.float32)
        query_labels = lax.dynamic_slice_in_dim(sorted_labels, offset, block_rows, 0)
        query_orders = lax.dynamic_slice_in_dim(sorted_orders, offset, block_rows, 0)
        key_labels = lax.dynamic_slice_in_dim(padded_labels, offset, reach + block_rows, 0)
        key_orders = lax.dynamic_slice_in_dim(padded_orders, offset, reach + block_rows, 0)
        allowed = (key_labels[None, :] == query_labels[:, None]) & (key_orders[None, :] < query_orders[:, None])
        return lax.optimization_barrier(jnp.max(jnp.where(allowed, scores, -1.0), axis=1))
    offsets = jnp.arange(total_rows // block_rows, dtype=jnp.int32) * block_rows
    sorted_maxima = lax.map(one_block, offsets).reshape(total_rows)
    return jnp.zeros((total_rows,), jnp.float32).at[sorting].set(sorted_maxima)
```

```python
import functools

import jax
import jax.numpy as jnp
from jax import lax
from jax.experimental import pallas as pl
from jax.experimental.pallas import tpu as pltpu
from jax.sharding import PartitionSpec as P

CL_DEV = 8
GROUPS = 4
HALF = GROUPS // 2
RANKS = 1024
LANES = 128
QUERY_TILE = 256

epsilon = 1e-06
floor_value = -1.0
MESH = pl.DeviceIdType.MESH
f32, bf16, i32 = jnp.float32, jnp.bfloat16, jnp.int32


def group_towards(group, half, shift):
    return lax.rem(group // HALF + half, 2) * HALF + lax.rem(group % HALF + shift, HALF)


def group_from(group, half, shift):
    return lax.rem(group // HALF + half, 2) * HALF + lax.rem(group % HALF + HALF - shift, HALF)


def group_place(source, target):
    half = (source // HALF + target // HALF) % 2
    shift = (target % HALF - source % HALF + HALF) % HALF
    return half * HALF + shift


def pieces_of(values):
    first = values.astype(bf16)
    left = values - first.astype(f32)
    second = left.astype(bf16)
    third = (left - second.astype(f32)).astype(bf16)
    return jnp.concatenate([first.astype(f32), second.astype(f32), third.astype(f32)], axis=0).astype(bf16)


def dot(left, right, contract):
    return lax.dot_general(left, right, (contract, ((), ())), preferred_element_type=f32)


def kernel(
    holders, pad,
    emb_hbm, cid_ref, rank_ref, out_ref,
    emb, outgoing, incoming, lab_out, lab_in, bias, best, ret, back,
    emb_sem, self_sem, lab_send, lab_recv, row_send, row_recv, ret_send, ret_recv,
):
    size = holders // GROUPS
    rows, features = emb.shape
    group_rows = size * pad
    total = holders * pad
    me = lax.axis_index("hold")
    my_group, my_spot = me // size, me % size

    fetch = pltpu.make_async_copy(emb_hbm, emb, emb_sem)
    fetch.start()

    barrier = pltpu.get_barrier_semaphore()

    def greet(step, carry):
        pl.semaphore_signal(
            barrier, inc=1, device_id={"hold": lax.rem(me + step, holders)}, device_id_type=MESH
        )
        return carry

    lax.fori_loop(1, holders, greet, 0)

    def place_of(source, target):
        return group_place(source // size, target // size) * size + source % size

    def spots(half, shift):
        return (1, size) if half == 0 and shift == 0 else (0, size)

    def target_of(half, shift, i):
        return group_towards(my_group, half, shift) * size + lax.rem(my_spot + i, size)

    def source_of(half, shift, i):
        return group_from(my_group, half, shift) * size + lax.rem(my_spot + i, size)

    kinds = [(1, 0), (1, 1), (0, 1), (0, 0)]

    def over(half, shift, body):
        start, end = spots(half, shift)

        def step(i, carry):
            body(i)
            return carry

        lax.fori_loop(start, end, step, 0, unroll=True if size <= 4 else 1)

    cid = cid_ref[...]
    owner = cid // CL_DEV
    code = (cid - owner * CL_DEV + 1) * RANKS + rank_ref[...]
    ids = lax.broadcasted_iota(i32, (holders, rows), 0)
    member = owner == ids
    member16 = jnp.where(member, 1.0, 0.0).astype(bf16)
    before = jnp.where(
        lax.broadcasted_iota(i32, (rows, rows), 0) < lax.broadcasted_iota(i32, (rows, rows), 1), 1.0, 0.0
    ).astype(bf16)
    earlier = dot(member16, before, ((1,), (0,)))
    nth = jnp.sum(jnp.where(member, earlier, 0.0), axis=0, keepdims=True).astype(i32)
    target = owner * pad + nth

    spread = jnp.where(lax.broadcasted_iota(i32, (LANES, rows), 0) == nth, 1.0, 0.0).astype(bf16)
    high = (code // 128).astype(f32)
    low = (code % 128).astype(f32)
    parts = jnp.concatenate(
        [jnp.where(member, high, 0.0), jnp.where(member, low, 0.0)], axis=0
    ).astype(bf16)
    packed = dot(parts, spread, ((1,), (1,)))
    labels = (packed[:holders] * 128.0 + packed[holders:]).astype(i32)
    for j in range(holders):
        lab_out[j] = labels[j : j + 1]

    pl.semaphore_wait(barrier, holders - 1)

    def label_copy(half, shift, i):
        dest = target_of(half, shift, i)
        place = place_of(me, dest)
        return pltpu.make_async_remote_copy(
            src_ref=lab_out.at[dest], dst_ref=lab_in.at[place],
            send_sem=lab_send.at[dest], recv_sem=lab_recv.at[place],
            device_id={"hold": dest}, device_id_type=MESH,
        )

    for half, shift in kinds:
        over(half, shift, lambda i: label_copy(half, shift, i).start())
    own_label = pltpu.make_async_copy(lab_out.at[me], lab_in.at[place_of(me, me)], self_sem.at[0])
    own_label.start()

    fetch.wait()
    x = emb[...]
    squares = jnp.sum(x * x, axis=1, keepdims=True)
    normed = (x * lax.rsqrt(squares + epsilon)).astype(bf16)

    def row_copy(number, half, shift, i):
        dest = target_of(half, shift, i)
        place = place_of(me, dest)
        return pltpu.make_async_remote_copy(
            src_ref=outgoing.at[number * size + dest % size], dst_ref=incoming.at[place],
            send_sem=row_send.at[dest], recv_sem=row_recv.at[place],
            device_id={"hold": dest}, device_id_type=MESH,
        )

    slot_ids = lax.broadcasted_iota(i32, (group_rows, rows), 0)
    for number, (half, shift) in enumerate(kinds):
        base = group_towards(my_group, half, shift) * group_rows
        chosen = jnp.where(slot_ids == target - base, 1.0, 0.0).astype(bf16)
        laid = dot(chosen, normed, ((1,), (0,))).astype(bf16)
        outgoing[number * size : (number + 1) * size] = laid.reshape(size, pad, features)
        over(half, shift, lambda i: row_copy(number, half, shift, i).start())
    own_rows = pltpu.make_async_copy(
        outgoing.at[(GROUPS - 1) * size + my_spot], incoming.at[place_of(me, me)], self_sem.at[1]
    )
    own_rows.start()

    windows = total // LANES - 2

    def window_of(place):
        return jnp.minimum(place * pad // LANES, windows)

    places = place_of(me, ids)
    starts = places * pad - window_of(places) * LANES
    lane = jnp.sum(jnp.where(member, starts, 0), axis=0, keepdims=True) + nth
    pick = jnp.where(lax.broadcasted_iota(i32, (2 * LANES, rows), 0) == lane, 1.0, 0.0).astype(bf16)

    for half, shift in kinds:
        over(half, shift, lambda i: label_copy(half, shift, i).wait_send())
    own_label.wait()

    def wait_labels(half, shift, i):
        place = place_of(source_of(half, shift, i), me)
        pltpu.make_async_remote_copy(
            src_ref=lab_out.at[me], dst_ref=lab_in.at[place],
            send_sem=lab_send.at[me], recv_sem=lab_recv.at[place],
            device_id={"hold": me}, device_id_type=MESH,
        ).wait_recv()

    for half, shift in kinds:
        over(half, shift, lambda i: wait_labels(half, shift, i))
    arrived = jnp.concatenate([lab_in[j] for j in range(holders)], axis=0)
    arrived = jnp.concatenate([(arrived // 128).astype(f32), (arrived % 128).astype(f32)], axis=0)
    widen = jnp.where(
        lax.broadcasted_iota(i32, (LANES, total), 1) % pad == lax.broadcasted_iota(i32, (LANES, total), 0),
        1.0, 0.0,
    ).astype(bf16)
    wide = dot(arrived.astype(bf16), widen, ((1,), (0,)))
    wide = wide[:holders] * 128.0 + wide[holders:]
    here = lax.broadcasted_iota(i32, (holders, total), 1) // pad == lax.broadcasted_iota(i32, (holders, total), 0)
    query = jnp.sum(jnp.where(here, wide, 0.0), axis=0, keepdims=True)
    query_first = jnp.floor(query * (1.0 / RANKS)) * RANKS
    key = jnp.transpose(jnp.broadcast_to(query, (LANES, total)))
    for tile in range(total // LANES):
        cut = slice(tile * LANES, (tile + 1) * LANES)
        allowed = (key < query[:, cut]) & (key >= query_first[:, cut])
        bias[:, cut] = jnp.where(allowed, 0.0, -4.0)

    def wait_rows(half, shift, i):
        place = place_of(source_of(half, shift, i), me)
        pltpu.make_async_remote_copy(
            src_ref=outgoing.at[0], dst_ref=incoming.at[place],
            send_sem=row_send.at[me], recv_sem=row_recv.at[place],
            device_id={"hold": me}, device_id_type=MESH,
        ).wait_recv()

    def rows_at(start, end):
        return incoming[start // pad : -(-end // pad)].reshape(-1, features)

    def tile_best(keys, first_key, last_key, queries, tile):
        cut = slice(tile * QUERY_TILE, (tile + 1) * QUERY_TILE)
        scores = dot(keys, queries, ((1,), (1,))) + bias[first_key:last_key, cut]
        return jnp.max(scores, axis=0, keepdims=True)

    early = (GROUPS - 1) * group_rows
    early_tiles = early // QUERY_TILE
    own_rows.wait()
    for half, shift in [(0, 0), (0, 1), (1, 0)]:
        over(half, shift, lambda i: wait_rows(half, shift, i))
    keys = incoming[: (GROUPS - 1) * size].reshape(early, features)
    for tile in range(early_tiles):
        queries = keys[tile * QUERY_TILE : (tile + 1) * QUERY_TILE]
        best[tile] = tile_best(keys, 0, early, queries, tile)
    over(1, 1, lambda i: wait_rows(1, 1, i))
    keys = incoming[...].reshape(total, features)
    for tile in range(total // QUERY_TILE):
        queries = keys[tile * QUERY_TILE : (tile + 1) * QUERY_TILE]
        if tile < early_tiles:
            most = jnp.maximum(best[tile], tile_best(keys[early:], early, total, queries, tile))
        else:
            most = tile_best(keys, 0, total, queries, tile)
        most = jnp.maximum(most, floor_value)
        for k in range(QUERY_TILE // LANES):
            ret[tile * (QUERY_TILE // LANES) + k] = most[:, k * LANES : (k + 1) * LANES]

    def ret_copy(half, shift, i):
        source = source_of(half, shift, i)
        return pltpu.make_async_remote_copy(
            src_ref=ret.at[pl.ds(window_of(place_of(source, me)), 2)], dst_ref=back.at[me],
            send_sem=ret_send.at[source], recv_sem=ret_recv.at[me],
            device_id={"hold": source}, device_id_type=MESH,
        )

    for half, shift in kinds:
        over(half, shift, lambda i: ret_copy(half, shift, i).start())
    own_ret = pltpu.make_async_copy(
        ret.at[pl.ds(window_of(place_of(me, me)), 2)], back.at[me], self_sem.at[2]
    )
    own_ret.start()
    for number, (half, shift) in enumerate(kinds):
        over(half, shift, lambda i: row_copy(number, half, shift, i).wait_send())

    def wait_ret(half, shift, i):
        dest = target_of(half, shift, i)
        pltpu.make_async_remote_copy(
            src_ref=ret.at[pl.ds(0, 2)], dst_ref=back.at[dest],
            send_sem=ret_send.at[me], recv_sem=ret_recv.at[dest],
            device_id={"hold": me}, device_id_type=MESH,
        ).wait_recv()

    own_ret.wait()
    for half, shift in kinds:
        over(half, shift, lambda i: wait_ret(half, shift, i))
    returned = jnp.concatenate(
        [jnp.concatenate([back[j, 0], back[j, 1]], axis=1) for j in range(holders)], axis=0
    )
    picked = dot(pieces_of(returned), pick, ((1,), (0,)))
    picked = picked[:holders] + picked[holders : 2 * holders] + picked[2 * holders :]
    out_ref[...] = jnp.sum(jnp.where(member, picked, 0.0), axis=0, keepdims=True)
    for half, shift in kinds:
        over(half, shift, lambda i: ret_copy(half, shift, i).wait_send())


def shards(embeddings, cluster_id, cluster_rank):
    holders = lax.axis_size("hold")
    rows, features = embeddings.shape
    slot_count = 3 * rows // (2 * holders)
    pad = -(-slot_count // 16) * 16
    total = holders * pad
    vmem = pl.BlockSpec(memory_space=pltpu.VMEM)
    out = pl.pallas_call(
        functools.partial(kernel, holders, pad),
        out_shape=jax.ShapeDtypeStruct((1, rows), f32),
        in_specs=[pl.BlockSpec(memory_space=pl.ANY), vmem, vmem],
        out_specs=vmem,
        scratch_shapes=[
            pltpu.VMEM((rows, features), f32),
            pltpu.VMEM((holders, pad, features), bf16),
            pltpu.VMEM((holders, pad, features), bf16),
            pltpu.VMEM((holders, 1, LANES), i32),
            pltpu.VMEM((holders, 1, LANES), i32),
            pltpu.VMEM((total, total), f32),
            pltpu.VMEM((total // QUERY_TILE, 1, QUERY_TILE), f32),
            pltpu.VMEM((total // LANES, 1, LANES), f32),
            pltpu.VMEM((holders, 2, 1, LANES), f32),
            pltpu.SemaphoreType.DMA,
            pltpu.SemaphoreType.DMA((3,)),
            pltpu.SemaphoreType.DMA((holders,)),
            pltpu.SemaphoreType.DMA((holders,)),
            pltpu.SemaphoreType.DMA((holders,)),
            pltpu.SemaphoreType.DMA((holders,)),
            pltpu.SemaphoreType.DMA((holders,)),
            pltpu.SemaphoreType.DMA((holders,)),
        ],
        compiler_params=pltpu.CompilerParams(
            collective_id=0, has_side_effects=True, vmem_limit_bytes=56 * 1024 * 1024
        ),
    )(embeddings, cluster_id.reshape(1, rows), cluster_rank.reshape(1, rows))
    return out.reshape(rows)


def solution(mesh):
    in_specs = (P(("parts", "hold"), None), P(("parts", "hold")), P(("parts", "hold")))
    out_specs = P(("parts", "hold"))
    return jax.shard_map(shards, mesh=mesh, in_specs=in_specs, out_specs=out_specs, check_vma=False)
```

```python
import functools

import jax
import jax.numpy as jnp
from jax import lax
from jax.experimental import pallas as pl
from jax.experimental.pallas import tpu as pltpu
from jax.sharding import PartitionSpec as P

CL_DEV = 8
GROUPS = 4
HALF = GROUPS // 2
RANKS = 1024
LANES = 128
QUERY_TILE = 256

epsilon = 1e-06
floor_value = -1.0
MESH = pl.DeviceIdType.MESH
f32, bf16, i32 = jnp.float32, jnp.bfloat16, jnp.int32


def group_towards(group, half, shift):
    return lax.rem(group // HALF + half, 2) * HALF + lax.rem(group % HALF + shift, HALF)


def group_from(group, half, shift):
    return lax.rem(group // HALF + half, 2) * HALF + lax.rem(group % HALF + HALF - shift, HALF)


def group_place(source, target):
    half = (source // HALF + target // HALF) % 2
    shift = (target % HALF - source % HALF + HALF) % HALF
    return half * HALF + shift


def pieces_of(values):
    first = values.astype(bf16)
    left = values - first.astype(f32)
    second = left.astype(bf16)
    third = (left - second.astype(f32)).astype(bf16)
    return jnp.concatenate([first.astype(f32), second.astype(f32), third.astype(f32)], axis=0).astype(bf16)


def dot(left, right, contract):
    return lax.dot_general(left, right, (contract, ((), ())), preferred_element_type=f32)


def kernel(
    holders, pad,
    emb_hbm, cid_hbm, rank_hbm, out_ref,
    cid_ref, rank_ref, emb, outgoing, incoming, lab_out, lab_in, bias, best, near, far, back,
    fetch_sem, self_sem, lab_send, lab_recv, row_send, row_recv, ret_send, ret_recv,
):
    size = holders // GROUPS
    rows, features = emb.shape
    group_rows = size * pad
    total = holders * pad
    me = lax.axis_index("hold")
    my_group, my_spot = me // size, me % size

    fetches = [
        pltpu.make_async_copy(src, dst, fetch_sem.at[n])
        for n, (src, dst) in enumerate([(cid_hbm, cid_ref), (rank_hbm, rank_ref), (emb_hbm, emb)])
    ]
    for fetch in fetches:
        fetch.start()

    barrier = pltpu.get_barrier_semaphore()

    def greet(step, carry):
        pl.semaphore_signal(
            barrier, inc=1, device_id={"hold": lax.rem(me + step, holders)}, device_id_type=MESH
        )
        return carry

    lax.fori_loop(1, holders, greet, 0)

    def place_of(source, target):
        return group_place(source // size, target // size) * size + source % size

    def spots(half, shift):
        return (1, size) if half == 0 and shift == 0 else (0, size)

    def target_of(half, shift, i):
        return group_towards(my_group, half, shift) * size + lax.rem(my_spot + i, size)

    def source_of(half, shift, i):
        return group_from(my_group, half, shift) * size + lax.rem(my_spot + i, size)

    kinds = [(1, 0), (1, 1), (0, 1), (0, 0)]

    def over(half, shift, body):
        start, end = spots(half, shift)

        def step(i, carry):
            body(i)
            return carry

        lax.fori_loop(start, end, step, 0, unroll=True if size <= 4 else 1)

    fetches[0].wait()
    cid = cid_ref[...]
    owner = cid // CL_DEV
    ids = lax.broadcasted_iota(i32, (holders, rows), 0)
    member = owner == ids
    member16 = jnp.where(member, 1.0, 0.0).astype(bf16)
    before = jnp.where(
        lax.broadcasted_iota(i32, (rows, rows), 0) < lax.broadcasted_iota(i32, (rows, rows), 1), 1.0, 0.0
    ).astype(bf16)
    earlier = dot(member16, before, ((1,), (0,)))
    nth = jnp.sum(jnp.where(member, earlier, 0.0), axis=0, keepdims=True).astype(i32)
    target = owner * pad + nth

    def label_copy(half, shift, i):
        dest = target_of(half, shift, i)
        place = place_of(me, dest)
        return pltpu.make_async_remote_copy(
            src_ref=lab_out.at[dest], dst_ref=lab_in.at[place],
            send_sem=lab_send.at[dest], recv_sem=lab_recv.at[place],
            device_id={"hold": dest}, device_id_type=MESH,
        )

    own_label = pltpu.make_async_copy(lab_out.at[me], lab_in.at[place_of(me, me)], self_sem.at[0])

    def send_labels():
        fetches[1].wait()
        code = (cid - owner * CL_DEV + 1) * RANKS + rank_ref[...]
        spread = jnp.where(lax.broadcasted_iota(i32, (LANES, rows), 0) == nth, 1.0, 0.0).astype(bf16)
        high = (code // 128).astype(f32)
        low = (code % 128).astype(f32)
        parts = jnp.concatenate(
            [jnp.where(member, high, 0.0), jnp.where(member, low, 0.0)], axis=0
        ).astype(bf16)
        packed = dot(parts, spread, ((1,), (1,)))
        labels = (packed[:holders] * 128.0 + packed[holders:]).astype(i32)
        for j in range(holders):
            lab_out[j] = labels[j : j + 1]
        for kind in kinds:
            over(*kind, lambda i: label_copy(*kind, i).start())
        own_label.start()

    fetches[2].wait()
    x = emb[...]
    squares = jnp.sum(x * x, axis=1, keepdims=True)
    normed = (x * lax.rsqrt(squares + epsilon)).astype(bf16)

    def row_copy(number, half, shift, i):
        dest = target_of(half, shift, i)
        place = place_of(me, dest)
        return pltpu.make_async_remote_copy(
            src_ref=outgoing.at[number * size + dest % size], dst_ref=incoming.at[place],
            send_sem=row_send.at[dest], recv_sem=row_recv.at[place],
            device_id={"hold": dest}, device_id_type=MESH,
        )

    slot_ids = lax.broadcasted_iota(i32, (group_rows, rows), 0)
    for number, (half, shift) in enumerate(kinds):
        base = group_towards(my_group, half, shift) * group_rows
        chosen = jnp.where(slot_ids == target - base, 1.0, 0.0).astype(bf16)
        laid = dot(chosen, normed, ((1,), (0,))).astype(bf16)
        outgoing[number * size : (number + 1) * size] = laid.reshape(size, pad, features)
        if number == 0:
            pl.semaphore_wait(barrier, holders - 1)
        over(half, shift, lambda i: row_copy(number, half, shift, i).start())
        if number == HALF - 1:
            send_labels()
    own_rows = pltpu.make_async_copy(
        outgoing.at[(GROUPS - 1) * size + my_spot], incoming.at[place_of(me, me)], self_sem.at[1]
    )
    own_rows.start()

    windows = total // LANES - 2

    def window_of(place):
        return jnp.minimum(place * pad // LANES, windows)

    places = place_of(me, ids)
    starts = places * pad - window_of(places) * LANES
    lane = jnp.sum(jnp.where(member, starts, 0), axis=0, keepdims=True) + nth
    pick = jnp.where(lax.broadcasted_iota(i32, (2 * LANES, rows), 0) == lane, 1.0, 0.0).astype(bf16)

    for half, shift in kinds:
        over(half, shift, lambda i: label_copy(half, shift, i).wait_send())
    own_label.wait()

    def wait_labels(half, shift, i):
        place = place_of(source_of(half, shift, i), me)
        pltpu.make_async_remote_copy(
            src_ref=lab_out.at[me], dst_ref=lab_in.at[place],
            send_sem=lab_send.at[me], recv_sem=lab_recv.at[place],
            device_id={"hold": me}, device_id_type=MESH,
        ).wait_recv()

    for half, shift in kinds:
        over(half, shift, lambda i: wait_labels(half, shift, i))
    arrived = jnp.concatenate([lab_in[j] for j in range(holders)], axis=0)
    arrived = jnp.concatenate([(arrived // 128).astype(f32), (arrived % 128).astype(f32)], axis=0)
    widen = jnp.where(
        lax.broadcasted_iota(i32, (LANES, total), 1) % pad == lax.broadcasted_iota(i32, (LANES, total), 0),
        1.0, 0.0,
    ).astype(bf16)
    wide = dot(arrived.astype(bf16), widen, ((1,), (0,)))
    wide = wide[:holders] * 128.0 + wide[holders:]
    here = lax.broadcasted_iota(i32, (holders, total), 1) // pad == lax.broadcasted_iota(i32, (holders, total), 0)
    query = jnp.sum(jnp.where(here, wide, 0.0), axis=0, keepdims=True)
    query_first = jnp.floor(query * (1.0 / RANKS)) * RANKS
    key = jnp.transpose(jnp.broadcast_to(query, (LANES, total)))
    for tile in range(total // LANES):
        cut = slice(tile * LANES, (tile + 1) * LANES)
        allowed = (key < query[:, cut]) & (key >= query_first[:, cut])
        bias[:, cut] = jnp.where(allowed, 0.0, -4.0)

    def wait_rows(half, shift, i):
        place = place_of(source_of(half, shift, i), me)
        pltpu.make_async_remote_copy(
            src_ref=outgoing.at[0], dst_ref=incoming.at[place],
            send_sem=row_send.at[me], recv_sem=row_recv.at[place],
            device_id={"hold": me}, device_id_type=MESH,
        ).wait_recv()

    def tile_best(keys, first_key, last_key, queries, tile):
        cut = slice(tile * QUERY_TILE, (tile + 1) * QUERY_TILE)
        scores = dot(keys, queries, ((1,), (1,))) + bias[first_key:last_key, cut]
        return jnp.max(scores, axis=0, keepdims=True)

    early = (GROUPS - 1) * group_rows
    early_tiles = early // QUERY_TILE
    own_rows.wait()
    for half, shift in [(0, 0), (0, 1), (1, 0)]:
        over(half, shift, lambda i: wait_rows(half, shift, i))
    keys = incoming[: (GROUPS - 1) * size].reshape(early, features)
    for tile in range(early_tiles):
        queries = keys[tile * QUERY_TILE : (tile + 1) * QUERY_TILE]
        best[tile] = tile_best(keys, 0, early, queries, tile)
    over(1, 1, lambda i: wait_rows(1, 1, i))
    keys = incoming[...].reshape(total, features)
    def ret_copy(half, shift, i):
        source = source_of(half, shift, i)
        bests = near if half == 0 else far
        return pltpu.make_async_remote_copy(
            src_ref=bests.at[pl.ds(window_of(place_of(source, me)), 2)], dst_ref=back.at[me],
            send_sem=ret_send.at[source], recv_sem=ret_recv.at[me],
            device_id={"hold": source}, device_id_type=MESH,
        )

    for tile in range(total // QUERY_TILE):
        queries = keys[tile * QUERY_TILE : (tile + 1) * QUERY_TILE]
        if tile < early_tiles:
            most = jnp.maximum(best[tile], tile_best(keys[early:], early, total, queries, tile))
        else:
            most = tile_best(keys, 0, total, queries, tile)
        most = jnp.maximum(most, floor_value)
        for k in range(QUERY_TILE // LANES):
            part = most[:, k * LANES : (k + 1) * LANES]
            number = tile * (QUERY_TILE // LANES) + k
            far[number] = part
            if tile < early_tiles:
                near[number] = part
        if tile == early_tiles - 1:
            for half, shift in [(0, 1), (0, 0)]:
                over(half, shift, lambda i: ret_copy(half, shift, i).start())
    for half, shift in [(1, 0), (1, 1)]:
        over(half, shift, lambda i: ret_copy(half, shift, i).start())
    own_ret = pltpu.make_async_copy(
        near.at[pl.ds(window_of(place_of(me, me)), 2)], back.at[me], self_sem.at[2]
    )
    own_ret.start()
    for number, (half, shift) in enumerate(kinds):
        over(half, shift, lambda i: row_copy(number, half, shift, i).wait_send())

    def wait_ret(half, shift, i):
        dest = target_of(half, shift, i)
        pltpu.make_async_remote_copy(
            src_ref=far.at[pl.ds(0, 2)], dst_ref=back.at[dest],
            send_sem=ret_send.at[me], recv_sem=ret_recv.at[dest],
            device_id={"hold": me}, device_id_type=MESH,
        ).wait_recv()

    own_ret.wait()
    for half, shift in kinds:
        over(half, shift, lambda i: wait_ret(half, shift, i))
    returned = jnp.concatenate(
        [jnp.concatenate([back[j, 0], back[j, 1]], axis=1) for j in range(holders)], axis=0
    )
    picked = dot(pieces_of(returned), pick, ((1,), (0,)))
    picked = picked[:holders] + picked[holders : 2 * holders] + picked[2 * holders :]
    out_ref[...] = jnp.sum(jnp.where(member, picked, 0.0), axis=0, keepdims=True)
    for half, shift in kinds:
        over(half, shift, lambda i: ret_copy(half, shift, i).wait_send())


def shards(embeddings, cluster_id, cluster_rank):
    holders = lax.axis_size("hold")
    rows, features = embeddings.shape
    slot_count = 3 * rows // (2 * holders)
    pad = -(-slot_count // 16) * 16
    total = holders * pad
    early_lanes = (GROUPS - 1) * (total // GROUPS) // QUERY_TILE * QUERY_TILE
    out = pl.pallas_call(
        functools.partial(kernel, holders, pad),
        out_shape=jax.ShapeDtypeStruct((1, rows), f32),
        in_specs=[pl.BlockSpec(memory_space=pl.ANY)] * 3,
        out_specs=pl.BlockSpec(memory_space=pltpu.VMEM),
        scratch_shapes=[
            pltpu.VMEM((1, rows), i32),
            pltpu.VMEM((1, rows), i32),
            pltpu.VMEM((rows, features), f32),
            pltpu.VMEM((holders, pad, features), bf16),
            pltpu.VMEM((holders, pad, features), bf16),
            pltpu.VMEM((holders, 1, LANES), i32),
            pltpu.VMEM((holders, 1, LANES), i32),
            pltpu.VMEM((total, total), f32),
            pltpu.VMEM((total // QUERY_TILE, 1, QUERY_TILE), f32),
            pltpu.VMEM((early_lanes // LANES, 1, LANES), f32),
            pltpu.VMEM((total // LANES, 1, LANES), f32),
            pltpu.VMEM((holders, 2, 1, LANES), f32),
            pltpu.SemaphoreType.DMA((3,)),
            pltpu.SemaphoreType.DMA((3,)),
            pltpu.SemaphoreType.DMA((holders,)),
            pltpu.SemaphoreType.DMA((holders,)),
            pltpu.SemaphoreType.DMA((holders,)),
            pltpu.SemaphoreType.DMA((holders,)),
            pltpu.SemaphoreType.DMA((holders,)),
            pltpu.SemaphoreType.DMA((holders,)),
        ],
        compiler_params=pltpu.CompilerParams(
            collective_id=0, has_side_effects=True, vmem_limit_bytes=56 * 1024 * 1024
        ),
    )(embeddings, cluster_id.reshape(1, rows), cluster_rank.reshape(1, rows))
    return out.reshape(rows)


def solution(mesh):
    in_specs = (P(("parts", "hold"), None), P(("parts", "hold")), P(("parts", "hold")))
    out_specs = P(("parts", "hold"))
    return jax.shard_map(shards, mesh=mesh, in_specs=in_specs, out_specs=out_specs, check_vma=False)
```

```python
import functools

import jax
import jax.numpy as jnp
from jax import lax
from jax.experimental import pallas as pl
from jax.experimental.pallas import tpu as pltpu
from jax.sharding import PartitionSpec as P

CL_DEV = 8
GROUPS = 4
HALF = GROUPS // 2
RANKS = 1024
LANES = 128
QUERY_TILE = 256

epsilon = 1e-06
floor_value = -1.0
MESH = pl.DeviceIdType.MESH
f32, bf16, i32 = jnp.float32, jnp.bfloat16, jnp.int32


def group_towards(group, half, shift):
    return lax.rem(group // HALF + half, 2) * HALF + lax.rem(group % HALF + shift, HALF)


def group_from(group, half, shift):
    return lax.rem(group // HALF + half, 2) * HALF + lax.rem(group % HALF + HALF - shift, HALF)


def group_place(source, target):
    half = (source // HALF + target // HALF) % 2
    shift = (target % HALF - source % HALF + HALF) % HALF
    return half * HALF + shift


def pieces_of(values):
    first = values.astype(bf16)
    left = values - first.astype(f32)
    second = left.astype(bf16)
    third = (left - second.astype(f32)).astype(bf16)
    return jnp.concatenate([first.astype(f32), second.astype(f32), third.astype(f32)], axis=0).astype(bf16)


def dot(left, right, contract):
    return lax.dot_general(left, right, (contract, ((), ())), preferred_element_type=f32)


def kernel(
    holders, pad,
    emb_hbm, cid_hbm, rank_hbm, out_ref,
    cid_ref, rank_ref, emb, outgoing, incoming, lab_out, lab_in, bias, best, near, far, back,
    fetch_sem, self_sem, lab_send, lab_recv, row_send, row_recv, ret_send, ret_recv,
):
    size = holders // GROUPS
    rows, features = emb.shape
    group_rows = size * pad
    total = holders * pad
    me = lax.axis_index("hold")
    my_group, my_spot = me // size, me % size

    fetches = [
        pltpu.make_async_copy(src, dst, fetch_sem.at[n])
        for n, (src, dst) in enumerate([(cid_hbm, cid_ref), (rank_hbm, rank_ref), (emb_hbm, emb)])
    ]
    for fetch in fetches:
        fetch.start()

    barrier = pltpu.get_barrier_semaphore()

    def greet(step, carry):
        pl.semaphore_signal(
            barrier, inc=1, device_id={"hold": lax.rem(me + step, holders)}, device_id_type=MESH
        )
        return carry

    lax.fori_loop(1, holders, greet, 0)

    def place_of(source, target):
        return group_place(source // size, target // size) * size + source % size

    def spots(half, shift):
        return (1, size) if half == 0 and shift == 0 else (0, size)

    def target_of(half, shift, i):
        return group_towards(my_group, half, shift) * size + lax.rem(my_spot + i, size)

    def source_of(half, shift, i):
        return group_from(my_group, half, shift) * size + lax.rem(my_spot + i, size)

    kinds = [(1, 0), (1, 1), (0, 1), (0, 0)]

    def over(half, shift, body):
        start, end = spots(half, shift)

        def step(i, carry):
            body(i)
            return carry

        lax.fori_loop(start, end, step, 0, unroll=True if size <= 4 else 1)

    fetches[0].wait()
    cid = cid_ref[...]
    owner = cid // CL_DEV
    ids = lax.broadcasted_iota(i32, (holders, rows), 0)
    member = owner == ids
    member16 = jnp.where(member, 1.0, 0.0).astype(bf16)
    before = jnp.where(
        lax.broadcasted_iota(i32, (rows, rows), 0) < lax.broadcasted_iota(i32, (rows, rows), 1), 1.0, 0.0
    ).astype(bf16)
    earlier = dot(member16, before, ((1,), (0,)))
    nth = jnp.sum(jnp.where(member, earlier, 0.0), axis=0, keepdims=True).astype(i32)
    target = owner * pad + nth

    def label_copy(half, shift, i):
        dest = target_of(half, shift, i)
        place = place_of(me, dest)
        return pltpu.make_async_remote_copy(
            src_ref=lab_out.at[dest], dst_ref=lab_in.at[place],
            send_sem=lab_send.at[dest], recv_sem=lab_recv.at[place],
            device_id={"hold": dest}, device_id_type=MESH,
        )

    own_label = pltpu.make_async_copy(lab_out.at[me], lab_in.at[place_of(me, me)], self_sem.at[0])

    def send_labels():
        fetches[1].wait()
        code = (cid - owner * CL_DEV + 1) * RANKS + rank_ref[...]
        spread = jnp.where(lax.broadcasted_iota(i32, (LANES, rows), 0) == nth, 1.0, 0.0).astype(bf16)
        high = (code // 128).astype(f32)
        low = (code % 128).astype(f32)
        parts = jnp.concatenate(
            [jnp.where(member, high, 0.0), jnp.where(member, low, 0.0)], axis=0
        ).astype(bf16)
        packed = dot(parts, spread, ((1,), (1,)))
        labels = (packed[:holders] * 128.0 + packed[holders:]).astype(i32)
        for j in range(holders):
            lab_out[j] = labels[j : j + 1]
        for kind in kinds:
            over(*kind, lambda i: label_copy(*kind, i).start())
        own_label.start()

    fetches[2].wait()
    x = emb[...]
    squares = jnp.sum(x * x, axis=1, keepdims=True)
    normed = (x * lax.rsqrt(squares + epsilon)).astype(bf16)

    def row_copy(number, half, shift, i):
        dest = target_of(half, shift, i)
        place = place_of(me, dest)
        return pltpu.make_async_remote_copy(
            src_ref=outgoing.at[number * size + dest % size], dst_ref=incoming.at[place],
            send_sem=row_send.at[dest], recv_sem=row_recv.at[place],
            device_id={"hold": dest}, device_id_type=MESH,
        )

    slot_ids = lax.broadcasted_iota(i32, (group_rows, rows), 0)
    for number, (half, shift) in enumerate(kinds):
        base = group_towards(my_group, half, shift) * group_rows
        chosen = jnp.where(slot_ids == target - base, 1.0, 0.0).astype(bf16)
        laid = dot(chosen, normed, ((1,), (0,))).astype(bf16)
        outgoing[number * size : (number + 1) * size] = laid.reshape(size, pad, features)
        if number == 0:
            pl.semaphore_wait(barrier, holders - 1)
        over(half, shift, lambda i: row_copy(number, half, shift, i).start())
        if number == 0:
            send_labels()
    own_rows = pltpu.make_async_copy(
        outgoing.at[(GROUPS - 1) * size + my_spot], incoming.at[place_of(me, me)], self_sem.at[1]
    )
    own_rows.start()

    windows = total // LANES - 2

    def window_of(place):
        return jnp.minimum(place * pad // LANES, windows)

    places = place_of(me, ids)
    starts = places * pad - window_of(places) * LANES
    lane = jnp.sum(jnp.where(member, starts, 0), axis=0, keepdims=True) + nth
    pick = jnp.where(lax.broadcasted_iota(i32, (2 * LANES, rows), 0) == lane, 1.0, 0.0).astype(bf16)

    for half, shift in kinds:
        over(half, shift, lambda i: label_copy(half, shift, i).wait_send())
    own_label.wait()

    def wait_labels(half, shift, i):
        place = place_of(source_of(half, shift, i), me)
        pltpu.make_async_remote_copy(
            src_ref=lab_out.at[me], dst_ref=lab_in.at[place],
            send_sem=lab_send.at[me], recv_sem=lab_recv.at[place],
            device_id={"hold": me}, device_id_type=MESH,
        ).wait_recv()

    for half, shift in kinds:
        over(half, shift, lambda i: wait_labels(half, shift, i))
    arrived = jnp.concatenate([lab_in[j] for j in range(holders)], axis=0)
    arrived = jnp.concatenate([(arrived // 128).astype(f32), (arrived % 128).astype(f32)], axis=0)
    widen = jnp.where(
        lax.broadcasted_iota(i32, (LANES, total), 1) % pad == lax.broadcasted_iota(i32, (LANES, total), 0),
        1.0, 0.0,
    ).astype(bf16)
    wide = dot(arrived.astype(bf16), widen, ((1,), (0,)))
    wide = wide[:holders] * 128.0 + wide[holders:]
    here = lax.broadcasted_iota(i32, (holders, total), 1) // pad == lax.broadcasted_iota(i32, (holders, total), 0)
    query = jnp.sum(jnp.where(here, wide, 0.0), axis=0, keepdims=True)
    query_first = jnp.floor(query * (1.0 / RANKS)) * RANKS
    key = jnp.transpose(jnp.broadcast_to(query, (LANES, total)))
    for tile in range(total // LANES):
        cut = slice(tile * LANES, (tile + 1) * LANES)
        allowed = (key < query[:, cut]) & (key >= query_first[:, cut])
        bias[:, cut] = jnp.where(allowed, 0.0, -4.0)

    def wait_rows(half, shift, i):
        place = place_of(source_of(half, shift, i), me)
        pltpu.make_async_remote_copy(
            src_ref=outgoing.at[0], dst_ref=incoming.at[place],
            send_sem=row_send.at[me], recv_sem=row_recv.at[place],
            device_id={"hold": me}, device_id_type=MESH,
        ).wait_recv()

    def tile_best(keys, first_key, last_key, queries, tile):
        cut = slice(tile * QUERY_TILE, (tile + 1) * QUERY_TILE)
        scores = dot(keys, queries, ((1,), (1,))) + bias[first_key:last_key, cut]
        return jnp.max(scores, axis=0, keepdims=True)

    early = (GROUPS - 1) * group_rows
    early_tiles = early // QUERY_TILE
    own_rows.wait()
    for half, shift in [(0, 0), (0, 1), (1, 0)]:
        over(half, shift, lambda i: wait_rows(half, shift, i))
    keys = incoming[: (GROUPS - 1) * size].reshape(early, features)
    for tile in range(early_tiles):
        queries = keys[tile * QUERY_TILE : (tile + 1) * QUERY_TILE]
        best[tile] = tile_best(keys, 0, early, queries, tile)
    over(1, 1, lambda i: wait_rows(1, 1, i))
    keys = incoming[...].reshape(total, features)
    def ret_copy(half, shift, i):
        source = source_of(half, shift, i)
        bests = near if half == 0 else far
        return pltpu.make_async_remote_copy(
            src_ref=bests.at[pl.ds(window_of(place_of(source, me)), 2)], dst_ref=back.at[me],
            send_sem=ret_send.at[source], recv_sem=ret_recv.at[me],
            device_id={"hold": source}, device_id_type=MESH,
        )

    for tile in range(total // QUERY_TILE):
        queries = keys[tile * QUERY_TILE : (tile + 1) * QUERY_TILE]
        if tile < early_tiles:
            most = jnp.maximum(best[tile], tile_best(keys[early:], early, total, queries, tile))
        else:
            most = tile_best(keys, 0, total, queries, tile)
        most = jnp.maximum(most, floor_value)
        for k in range(QUERY_TILE // LANES):
            part = most[:, k * LANES : (k + 1) * LANES]
            number = tile * (QUERY_TILE // LANES) + k
            far[number] = part
            if tile < early_tiles:
                near[number] = part
        if tile == early_tiles - 1:
            for half, shift in [(0, 1), (0, 0)]:
                over(half, shift, lambda i: ret_copy(half, shift, i).start())
    for half, shift in [(1, 0), (1, 1)]:
        over(half, shift, lambda i: ret_copy(half, shift, i).start())
    own_ret = pltpu.make_async_copy(
        near.at[pl.ds(window_of(place_of(me, me)), 2)], back.at[me], self_sem.at[2]
    )
    own_ret.start()
    for number, (half, shift) in enumerate(kinds):
        over(half, shift, lambda i: row_copy(number, half, shift, i).wait_send())

    def wait_ret(half, shift, i):
        dest = target_of(half, shift, i)
        pltpu.make_async_remote_copy(
            src_ref=far.at[pl.ds(0, 2)], dst_ref=back.at[dest],
            send_sem=ret_send.at[me], recv_sem=ret_recv.at[dest],
            device_id={"hold": me}, device_id_type=MESH,
        ).wait_recv()

    own_ret.wait()
    for half, shift in kinds:
        over(half, shift, lambda i: wait_ret(half, shift, i))
    returned = jnp.concatenate(
        [jnp.concatenate([back[j, 0], back[j, 1]], axis=1) for j in range(holders)], axis=0
    )
    picked = dot(pieces_of(returned), pick, ((1,), (0,)))
    picked = picked[:holders] + picked[holders : 2 * holders] + picked[2 * holders :]
    out_ref[...] = jnp.sum(jnp.where(member, picked, 0.0), axis=0, keepdims=True)
    for half, shift in kinds:
        over(half, shift, lambda i: ret_copy(half, shift, i).wait_send())


def shards(embeddings, cluster_id, cluster_rank):
    holders = lax.axis_size("hold")
    rows, features = embeddings.shape
    slot_count = 3 * rows // (2 * holders)
    pad = -(-slot_count // 16) * 16
    total = holders * pad
    early_lanes = (GROUPS - 1) * (total // GROUPS) // QUERY_TILE * QUERY_TILE
    out = pl.pallas_call(
        functools.partial(kernel, holders, pad),
        out_shape=jax.ShapeDtypeStruct((1, rows), f32),
        in_specs=[pl.BlockSpec(memory_space=pl.ANY)] * 3,
        out_specs=pl.BlockSpec(memory_space=pltpu.VMEM),
        scratch_shapes=[
            pltpu.VMEM((1, rows), i32),
            pltpu.VMEM((1, rows), i32),
            pltpu.VMEM((rows, features), f32),
            pltpu.VMEM((holders, pad, features), bf16),
            pltpu.VMEM((holders, pad, features), bf16),
            pltpu.VMEM((holders, 1, LANES), i32),
            pltpu.VMEM((holders, 1, LANES), i32),
            pltpu.VMEM((total, total), f32),
            pltpu.VMEM((total // QUERY_TILE, 1, QUERY_TILE), f32),
            pltpu.VMEM((early_lanes // LANES, 1, LANES), f32),
            pltpu.VMEM((total // LANES, 1, LANES), f32),
            pltpu.VMEM((holders, 2, 1, LANES), f32),
            pltpu.SemaphoreType.DMA((3,)),
            pltpu.SemaphoreType.DMA((3,)),
            pltpu.SemaphoreType.DMA((holders,)),
            pltpu.SemaphoreType.DMA((holders,)),
            pltpu.SemaphoreType.DMA((holders,)),
            pltpu.SemaphoreType.DMA((holders,)),
            pltpu.SemaphoreType.DMA((holders,)),
            pltpu.SemaphoreType.DMA((holders,)),
        ],
        compiler_params=pltpu.CompilerParams(
            collective_id=0, has_side_effects=True, vmem_limit_bytes=56 * 1024 * 1024
        ),
    )(embeddings, cluster_id.reshape(1, rows), cluster_rank.reshape(1, rows))
    return out.reshape(rows)


def solution(mesh):
    in_specs = (P(("parts", "hold"), None), P(("parts", "hold")), P(("parts", "hold")))
    out_specs = P(("parts", "hold"))
    return jax.shard_map(shards, mesh=mesh, in_specs=in_specs, out_specs=out_specs, check_vma=False)
```

```python
import functools

import jax
import jax.numpy as jnp
from jax import lax
from jax.experimental import pallas as pl
from jax.experimental.pallas import tpu as pltpu
from jax.sharding import PartitionSpec as P

CL_DEV = 8
GROUPS = 4
HALF = GROUPS // 2
RANKS = 1024
LANES = 128
QUERY_TILE = 256

epsilon = 1e-06
floor_value = -1.0
MESH = pl.DeviceIdType.MESH
f32, bf16, i32 = jnp.float32, jnp.bfloat16, jnp.int32


def group_towards(group, half, shift):
    return lax.rem(group // HALF + half, 2) * HALF + lax.rem(group % HALF + shift, HALF)


def group_from(group, half, shift):
    return lax.rem(group // HALF + half, 2) * HALF + lax.rem(group % HALF + HALF - shift, HALF)


def group_place(source, target):
    half = (source // HALF + target // HALF) % 2
    shift = (target % HALF - source % HALF + HALF) % HALF
    return half * HALF + shift


def pieces_of(values):
    first = values.astype(bf16)
    left = values - first.astype(f32)
    second = left.astype(bf16)
    third = (left - second.astype(f32)).astype(bf16)
    return jnp.concatenate([first.astype(f32), second.astype(f32), third.astype(f32)], axis=0).astype(bf16)


def dot(left, right, contract):
    return lax.dot_general(left, right, (contract, ((), ())), preferred_element_type=f32)


def kernel(
    holders, pad,
    emb_hbm, cid_hbm, rank_hbm, out_ref,
    cid_ref, rank_ref, emb, outgoing, incoming, lab_out, lab_in, bias, best, near, far, back,
    fetch_sem, self_sem, lab_send, lab_recv, row_send, row_recv, ret_send, ret_recv,
):
    size = holders // GROUPS
    rows, features = emb.shape
    group_rows = size * pad
    total = holders * pad
    me = lax.axis_index("hold")
    my_group, my_spot = me // size, me % size

    fetches = [
        pltpu.make_async_copy(src, dst, fetch_sem.at[n])
        for n, (src, dst) in enumerate([(cid_hbm, cid_ref), (rank_hbm, rank_ref), (emb_hbm, emb)])
    ]

    barrier = pltpu.get_barrier_semaphore()

    def greet(step, carry):
        pl.semaphore_signal(
            barrier, inc=1, device_id={"hold": lax.rem(me + step, holders)}, device_id_type=MESH
        )
        return carry

    lax.fori_loop(1, holders, greet, 0)
    for fetch in fetches:
        fetch.start()

    def place_of(source, target):
        return group_place(source // size, target // size) * size + source % size

    def spots(half, shift):
        return (1, size) if half == 0 and shift == 0 else (0, size)

    def target_of(half, shift, i):
        return group_towards(my_group, half, shift) * size + lax.rem(my_spot + i, size)

    def source_of(half, shift, i):
        return group_from(my_group, half, shift) * size + lax.rem(my_spot + i, size)

    kinds = [(1, 0), (1, 1), (0, 1), (0, 0)]

    def over(half, shift, body):
        start, end = spots(half, shift)

        def step(i, carry):
            body(i)
            return carry

        lax.fori_loop(start, end, step, 0, unroll=True if size <= 4 else 1)

    fetches[0].wait()
    cid = cid_ref[...]
    owner = cid // CL_DEV
    ids = lax.broadcasted_iota(i32, (holders, rows), 0)
    member = owner == ids
    member16 = jnp.where(member, 1.0, 0.0).astype(bf16)
    before = jnp.where(
        lax.broadcasted_iota(i32, (rows, rows), 0) < lax.broadcasted_iota(i32, (rows, rows), 1), 1.0, 0.0
    ).astype(bf16)
    earlier = dot(member16, before, ((1,), (0,)))
    nth = jnp.sum(jnp.where(member, earlier, 0.0), axis=0, keepdims=True).astype(i32)
    target = owner * pad + nth

    def label_copy(half, shift, i):
        dest = target_of(half, shift, i)
        place = place_of(me, dest)
        return pltpu.make_async_remote_copy(
            src_ref=lab_out.at[dest], dst_ref=lab_in.at[place],
            send_sem=lab_send.at[dest], recv_sem=lab_recv.at[place],
            device_id={"hold": dest}, device_id_type=MESH,
        )

    own_label = pltpu.make_async_copy(lab_out.at[me], lab_in.at[place_of(me, me)], self_sem.at[0])

    def send_labels():
        fetches[1].wait()
        code = (cid - owner * CL_DEV + 1) * RANKS + rank_ref[...]
        spread = jnp.where(lax.broadcasted_iota(i32, (LANES, rows), 0) == nth, 1.0, 0.0).astype(bf16)
        high = (code // 128).astype(f32)
        low = (code % 128).astype(f32)
        parts = jnp.concatenate(
            [jnp.where(member, high, 0.0), jnp.where(member, low, 0.0)], axis=0
        ).astype(bf16)
        packed = dot(parts, spread, ((1,), (1,)))
        labels = (packed[:holders] * 128.0 + packed[holders:]).astype(i32)
        for j in range(holders):
            lab_out[j] = labels[j : j + 1]
        for kind in kinds:
            over(*kind, lambda i: label_copy(*kind, i).start())
        own_label.start()

    fetches[2].wait()
    x = emb[...]
    squares = jnp.sum(x * x, axis=1, keepdims=True)
    normed = (x * lax.rsqrt(squares + epsilon)).astype(bf16)

    def row_copy(number, half, shift, i):
        dest = target_of(half, shift, i)
        place = place_of(me, dest)
        return pltpu.make_async_remote_copy(
            src_ref=outgoing.at[number * size + dest % size], dst_ref=incoming.at[place],
            send_sem=row_send.at[dest], recv_sem=row_recv.at[place],
            device_id={"hold": dest}, device_id_type=MESH,
        )

    slot_ids = lax.broadcasted_iota(i32, (group_rows, rows), 0)
    for number, (half, shift) in enumerate(kinds):
        base = group_towards(my_group, half, shift) * group_rows
        chosen = jnp.where(slot_ids == target - base, 1.0, 0.0).astype(bf16)
        laid = dot(chosen, normed, ((1,), (0,))).astype(bf16)
        outgoing[number * size : (number + 1) * size] = laid.reshape(size, pad, features)
        if number == 0:
            pl.semaphore_wait(barrier, holders - 1)
        over(half, shift, lambda i: row_copy(number, half, shift, i).start())
        if number == 0:
            send_labels()
    own_rows = pltpu.make_async_copy(
        outgoing.at[(GROUPS - 1) * size + my_spot], incoming.at[place_of(me, me)], self_sem.at[1]
    )
    own_rows.start()

    windows = total // LANES - 2

    def window_of(place):
        return jnp.minimum(place * pad // LANES, windows)

    places = place_of(me, ids)
    starts = places * pad - window_of(places) * LANES
    lane = jnp.sum(jnp.where(member, starts, 0), axis=0, keepdims=True) + nth
    pick = jnp.where(lax.broadcasted_iota(i32, (2 * LANES, rows), 0) == lane, 1.0, 0.0).astype(bf16)

    for half, shift in kinds:
        over(half, shift, lambda i: label_copy(half, shift, i).wait_send())
    own_label.wait()

    def wait_labels(half, shift, i):
        place = place_of(source_of(half, shift, i), me)
        pltpu.make_async_remote_copy(
            src_ref=lab_out.at[me], dst_ref=lab_in.at[place],
            send_sem=lab_send.at[me], recv_sem=lab_recv.at[place],
            device_id={"hold": me}, device_id_type=MESH,
        ).wait_recv()

    for half, shift in kinds:
        over(half, shift, lambda i: wait_labels(half, shift, i))
    arrived = jnp.concatenate([lab_in[j] for j in range(holders)], axis=0)
    arrived = jnp.concatenate([(arrived // 128).astype(f32), (arrived % 128).astype(f32)], axis=0)
    widen = jnp.where(
        lax.broadcasted_iota(i32, (LANES, total), 1) % pad == lax.broadcasted_iota(i32, (LANES, total), 0),
        1.0, 0.0,
    ).astype(bf16)
    wide = dot(arrived.astype(bf16), widen, ((1,), (0,)))
    wide = wide[:holders] * 128.0 + wide[holders:]
    here = lax.broadcasted_iota(i32, (holders, total), 1) // pad == lax.broadcasted_iota(i32, (holders, total), 0)
    query = jnp.sum(jnp.where(here, wide, 0.0), axis=0, keepdims=True)
    query_first = jnp.floor(query * (1.0 / RANKS)) * RANKS
    key = jnp.transpose(jnp.broadcast_to(query, (LANES, total)))
    for tile in range(total // LANES):
        cut = slice(tile * LANES, (tile + 1) * LANES)
        allowed = (key < query[:, cut]) & (key >= query_first[:, cut])
        bias[:, cut] = jnp.where(allowed, 0.0, -4.0)

    def wait_rows(half, shift, i):
        place = place_of(source_of(half, shift, i), me)
        pltpu.make_async_remote_copy(
            src_ref=outgoing.at[0], dst_ref=incoming.at[place],
            send_sem=row_send.at[me], recv_sem=row_recv.at[place],
            device_id={"hold": me}, device_id_type=MESH,
        ).wait_recv()

    def tile_best(keys, first_key, last_key, queries, tile):
        cut = slice(tile * QUERY_TILE, (tile + 1) * QUERY_TILE)
        scores = dot(keys, queries, ((1,), (1,))) + bias[first_key:last_key, cut]
        return jnp.max(scores, axis=0, keepdims=True)

    early = (GROUPS - 1) * group_rows
    early_tiles = early // QUERY_TILE
    own_rows.wait()
    for half, shift in [(0, 0), (0, 1), (1, 0)]:
        over(half, shift, lambda i: wait_rows(half, shift, i))
    keys = incoming[: (GROUPS - 1) * size].reshape(early, features)
    for tile in range(early_tiles):
        queries = keys[tile * QUERY_TILE : (tile + 1) * QUERY_TILE]
        best[tile] = tile_best(keys, 0, early, queries, tile)
    over(1, 1, lambda i: wait_rows(1, 1, i))
    keys = incoming[...].reshape(total, features)
    def ret_copy(half, shift, i):
        source = source_of(half, shift, i)
        bests = near if half == 0 else far
        return pltpu.make_async_remote_copy(
            src_ref=bests.at[pl.ds(window_of(place_of(source, me)), 2)], dst_ref=back.at[me],
            send_sem=ret_send.at[source], recv_sem=ret_recv.at[me],
            device_id={"hold": source}, device_id_type=MESH,
        )

    for tile in range(total // QUERY_TILE):
        queries = keys[tile * QUERY_TILE : (tile + 1) * QUERY_TILE]
        if tile < early_tiles:
            most = jnp.maximum(best[tile], tile_best(keys[early:], early, total, queries, tile))
        else:
            most = tile_best(keys, 0, total, queries, tile)
        most = jnp.maximum(most, floor_value)
        for k in range(QUERY_TILE // LANES):
            part = most[:, k * LANES : (k + 1) * LANES]
            number = tile * (QUERY_TILE // LANES) + k
            far[number] = part
            if tile < early_tiles:
                near[number] = part
        if tile == early_tiles - 1:
            for half, shift in [(0, 1), (0, 0)]:
                over(half, shift, lambda i: ret_copy(half, shift, i).start())
    for half, shift in [(1, 0), (1, 1)]:
        over(half, shift, lambda i: ret_copy(half, shift, i).start())
    own_ret = pltpu.make_async_copy(
        near.at[pl.ds(window_of(place_of(me, me)), 2)], back.at[me], self_sem.at[2]
    )
    own_ret.start()

    def wait_ret(half, shift, i):
        dest = target_of(half, shift, i)
        pltpu.make_async_remote_copy(
            src_ref=far.at[pl.ds(0, 2)], dst_ref=back.at[dest],
            send_sem=ret_send.at[me], recv_sem=ret_recv.at[dest],
            device_id={"hold": me}, device_id_type=MESH,
        ).wait_recv()

    own_ret.wait()
    for half, shift in kinds:
        over(half, shift, lambda i: wait_ret(half, shift, i))
    returned = jnp.concatenate(
        [jnp.concatenate([back[j, 0], back[j, 1]], axis=1) for j in range(holders)], axis=0
    )
    picked = dot(pieces_of(returned), pick, ((1,), (0,)))
    picked = picked[:holders] + picked[holders : 2 * holders] + picked[2 * holders :]
    out_ref[...] = jnp.sum(jnp.where(member, picked, 0.0), axis=0, keepdims=True)
    for half, shift in kinds:
        over(half, shift, lambda i: ret_copy(half, shift, i).wait_send())
    for number, (half, shift) in enumerate(kinds):
        over(half, shift, lambda i: row_copy(number, half, shift, i).wait_send())


def shards(embeddings, cluster_id, cluster_rank):
    holders = lax.axis_size("hold")
    rows, features = embeddings.shape
    slot_count = 3 * rows // (2 * holders)
    pad = -(-slot_count // 16) * 16
    total = holders * pad
    early_lanes = (GROUPS - 1) * (total // GROUPS) // QUERY_TILE * QUERY_TILE
    out = pl.pallas_call(
        functools.partial(kernel, holders, pad),
        out_shape=jax.ShapeDtypeStruct((1, rows), f32),
        in_specs=[pl.BlockSpec(memory_space=pl.ANY)] * 3,
        out_specs=pl.BlockSpec(memory_space=pltpu.VMEM),
        scratch_shapes=[
            pltpu.VMEM((1, rows), i32),
            pltpu.VMEM((1, rows), i32),
            pltpu.VMEM((rows, features), f32),
            pltpu.VMEM((holders, pad, features), bf16),
            pltpu.VMEM((holders, pad, features), bf16),
            pltpu.VMEM((holders, 1, LANES), i32),
            pltpu.VMEM((holders, 1, LANES), i32),
            pltpu.VMEM((total, total), f32),
            pltpu.VMEM((total // QUERY_TILE, 1, QUERY_TILE), f32),
            pltpu.VMEM((early_lanes // LANES, 1, LANES), f32),
            pltpu.VMEM((total // LANES, 1, LANES), f32),
            pltpu.VMEM((holders, 2, 1, LANES), f32),
            pltpu.SemaphoreType.DMA((3,)),
            pltpu.SemaphoreType.DMA((3,)),
            pltpu.SemaphoreType.DMA((holders,)),
            pltpu.SemaphoreType.DMA((holders,)),
            pltpu.SemaphoreType.DMA((holders,)),
            pltpu.SemaphoreType.DMA((holders,)),
            pltpu.SemaphoreType.DMA((holders,)),
            pltpu.SemaphoreType.DMA((holders,)),
        ],
        compiler_params=pltpu.CompilerParams(
            collective_id=0, has_side_effects=True, vmem_limit_bytes=56 * 1024 * 1024
        ),
    )(embeddings, cluster_id.reshape(1, rows), cluster_rank.reshape(1, rows))
    return out.reshape(rows)


def solution(mesh):
    in_specs = (P(("parts", "hold"), None), P(("parts", "hold")), P(("parts", "hold")))
    out_specs = P(("parts", "hold"))
    return jax.shard_map(shards, mesh=mesh, in_specs=in_specs, out_specs=out_specs, check_vma=False)
```
